256 devices in a mesh: row: 2 (over core), col: 8 (over z), depth: 16 (over y, x).
Axes of the slice: x: 4, y: 4, z: 8, core: 2. Of those that a mesh axis runs over, the one named last changes fastest.
Arguments:
- gram_slab: float32 [32, 2, 256, 2, 8, 256], P(None, 'row', None, None, 'col'), may hold values from -1537 to 2561, as said below
Outputs:
- factored: float32 [32, 2, 256, 2, 8, 256], P('depth', 'row', None, None, 'col')
The draws below stay inside these ranges and needn't reach their ends.
Inputs may be any that keep to these rules, and one draw needn't show every extreme that they name: `gram_slab`: the top 4096 rows of S form a symmetric block, and its leading 2 * 256 rows and columns are positive definite.
All inputs are finite; a program needn't handle non-finite values.
Results may differ from the reference program's by a relative error of at most 0.0001.
Values sent between devices are 32-bit elements; how exact they have to be, the bound alone decides.
No kernel may reach another device: no remote copies, remote signals or barrier semaphores. Data moves between devices by JAX's collectives and lax.ppermute only.
A program may use at most 192 MiB of HBM per device.

```python
import jax
import jax.numpy as jnp
from jax import lax

NB = 256
ORDER = 16384
CT = 2
TR = 32
WIDTH = 4096
N_ROW = 2
N_COL = 8


def draw_gram_slab(key, part):
    key = jax.random.fold_in(key, 11)
    entry_key = jax.random.fold_in(key, 0)
    pivot_key = jax.random.fold_in(key, 2)
    link_key = jax.random.fold_in(key, 3)
    sign_key = jax.random.fold_in(key, 4)
    entries = jax.random.uniform(entry_key, (ORDER, WIDTH), jnp.float32, -1.0, 1.0)
    link_low = 3.0 * NB
    pivot_high = 10.0 * NB
    upper_block = entries[:WIDTH]
    upper_block = 0.5 * (upper_block + upper_block.T)
    entries = jnp.concatenate([upper_block, entries[WIDTH:]], axis=0)
    row_ids = jnp.arange(ORDER)[:, None]
    col_ids = jnp.arange(WIDTH)[None, :]
    leading = (row_ids < 2 * NB) & (col_ids < 2 * NB)
    row_scale = jnp.where(leading, 1.0, 8.0)
    pivots = jax.random.uniform(pivot_key, (ORDER, 1), jnp.float32, 8.0 * NB + 1.0, pivot_high)
    signs = 2.0 * jax.random.randint(sign_key, (NB,), 0, 2).astype(jnp.float32) - 1.0
    links = jax.random.uniform(link_key, (NB,), jnp.float32, link_low, 6.0 * NB) * signs
    link_rows = jnp.concatenate([links, jnp.zeros((ORDER - NB,), jnp.float32)])
    link_cols = jnp.concatenate([links, jnp.zeros((WIDTH - NB,), jnp.float32)])
    coupling = jnp.where(col_ids - row_ids == NB, link_rows[:, None], 0.0)
    coupling = coupling + jnp.where(row_ids - col_ids == NB, link_cols[None, :], 0.0)
    values = entries * row_scale + jnp.where((row_ids == col_ids) & leading, pivots, 0.0) + coupling
    return values.reshape(TR, ORDER // (TR * NB), NB, CT, WIDTH // (CT * NB), NB)


def setup_inputs(seed: int = 0) -> dict:
    arg_keys = jax.random.split(jax.random.key(seed), 2)
    gram_slab = draw_gram_slab(jax.random.fold_in(arg_keys[1], 71), 0)
    return {"gram_slab": gram_slab}


highest = lax.Precision.HIGHEST

def reference(gram_slab):
    current = gram_slab.reshape(ORDER, WIDTH)
    tile_index = (jnp.arange(ORDER) // NB).astype(jnp.int32)
    identity = jnp.eye(NB, dtype=current.dtype)
    panels = []
    for panel_id in range(2):
        left_edge = panel_id * NB
        right_edge = left_edge + NB
        column = current[:, left_edge:right_edge]
        pivot_block = column[left_edge:right_edge]
        factor = jnp.linalg.cholesky(pivot_block)
        inverse = jax.scipy.linalg.solve_triangular(factor, identity, lower=True)
        panel_block = jnp.dot(column, inverse.T, precision=highest, preferred_element_type=current.dtype)
        panel_block = jnp.where(tile_index[:, None] >= panel_id, panel_block, jnp.zeros_like(panel_block))
        panels.append(panel_block)
        lower_rows = jnp.where(tile_index[:, None] > panel_id, panel_block, jnp.zeros_like(panel_block))
        change = jnp.dot(lower_rows, panel_block[right_edge:WIDTH].T, precision=highest, preferred_element_type=current.dtype)
        current = current.at[:, right_edge:].add(-change)
    result = jnp.concatenate([panels[0], panels[1], current[:, 2 * NB:]], axis=1)
    return result.reshape(TR, N_ROW, NB, CT, N_COL, NB)
```

```python
import jax
import jax.numpy as jnp
from jax import lax
from jax.experimental import pallas as pl
from jax.experimental.pallas import tpu as pltpu
from jax.sharding import PartitionSpec as P

NB = 256
STEP = 32
SUB = 8
LANES = 128
highest = lax.Precision.HIGHEST


def dot(a, b, ca=1, cb=0):
    return lax.dot_general(
        a, b, (((ca,), (cb,)), ((), ())), precision=highest, preferred_element_type=jnp.float32
    )


def tile_from(ref):
    rows = ref.shape[0] // 2
    return jnp.concatenate([ref[pl.ds(0, rows, stride=2), :], ref[pl.ds(1, rows, stride=2), :]], axis=1)


def wide_from(ref):
    rows = ref.shape[0] // 4
    return jnp.concatenate([ref[pl.ds(q, rows, stride=4), :] for q in range(4)], axis=1)


def factor_panel(panel):
    groups = STEP // SUB
    lo = [panel[SUB * g : SUB * (g + 1), :LANES] for g in range(groups)]
    hi = [panel[SUB * g : SUB * (g + 1), LANES:] for g in range(groups)]
    shape = (SUB, LANES)
    lane = lax.broadcasted_iota(jnp.int32, shape, 1)
    sub = lax.broadcasted_iota(jnp.int32, shape, 0)
    for q in range(groups):
        live = range(q, groups)
        cols = [
            {g: jnp.broadcast_to(lo[g][:, SUB * q + j : SUB * q + j + 1], shape) for g in live}
            for j in range(SUB)
        ]
        d = {(i, j): jnp.broadcast_to(cols[j][q][i : i + 1, :], shape) for j in range(SUB) for i in range(j, SUB)}
        scale, low = [], {}
        for j in range(SUB):
            p = d[j, j]
            s = lax.rsqrt(p)
            scale.append(s)
            for i in range(j + 1, SUB):
                low[i, j] = d[i, j] * s
            for k in range(j + 1, SUB):
                for i in range(k, SUB):
                    d[i, k] = d[i, k] - low[i, j] * low[k, j]
        for j in range(SUB):
            s = scale[j]
            at = lane == SUB * q + j
            m = {g: cols[j][g] * s for g in live}
            for k in range(j + 1, SUB):
                for g in live:
                    cols[k][g] = cols[k][g] - m[g] * low[k, j]
            m[q] = jnp.where(sub > j, m[q], 0.0)
            row_lo = jnp.broadcast_to(lo[q][j : j + 1, :], shape)
            row_hi = jnp.broadcast_to(hi[q][j : j + 1, :], shape)
            u_lo = jnp.where(at, 1.0, row_lo) * s
            u_hi = row_hi * s
            for g in live:
                clear = at & (sub > j) if g == q else at
                lo[g] = jnp.where(clear, 0.0, lo[g]) - m[g] * u_lo
                hi[g] = hi[g] - m[g] * u_hi
            lo[q] = jnp.where(sub == j, u_lo, lo[q])
            hi[q] = jnp.where(sub == j, u_hi, hi[q])
    for g in range(groups):
        lo[g] = jnp.where((lane < STEP) & (lane > sub + SUB * g), 0.0, lo[g])
    return jnp.concatenate(
        [jnp.concatenate([lo[g], hi[g]], axis=1) for g in range(groups)], axis=0
    )


def factor(work, prev):
    row_id = lax.broadcasted_iota(jnp.int32, (NB, NB), 0)
    lane_id = lax.broadcasted_iota(jnp.int32, (NB, NB), 1)
    panel_lane = lax.broadcasted_iota(jnp.int32, (STEP, NB), 1)
    prev[...] = jnp.zeros((STEP, NB), jnp.float32)

    def body(step, carry):
        start = pl.multiple_of(step * STEP, STEP)
        stop = start + STEP
        turn = lax.rem(NB - start, NB)
        last = prev[...]
        rolled = pltpu.roll(last, turn, axis=1)
        panel = pltpu.roll(work[pl.ds(start, STEP), :], turn, axis=1)
        panel = jnp.where((panel_lane >= NB - STEP) & (step > 0), 0.0, panel)
        panel = panel - dot(rolled[:, :STEP], rolled, 0, 0)
        panel = pltpu.roll(factor_panel(panel), start, axis=1)
        below = jnp.where(panel_lane >= stop, last, 0.0)
        spent = (row_id >= stop) & (lane_id >= start - STEP) & (lane_id < start)
        work[...] = jnp.where(spent, 0.0, work[...]) - dot(below, last, 0, 0)
        work[pl.ds(start, STEP), :] = panel
        prev[...] = panel
        return carry

    lax.fori_loop(0, NB // STEP, body, 0)
    return jnp.where(lane_id <= row_id, work[...], 0.0)


def tiles_from(gathered, k, out):
    for d in range(16):
        out[pl.ds(16 * d, 16), :] = tile_from(gathered.at[d, k])


def first_kernel(ids, gathered, inv_ref, work, prev):
    tiles_from(gathered, 0, work)
    inv_ref[...] = factor(work, prev)


def second_kernel(ids, gathered, inv0_ref, up_ref, inv_ref, work, prev):
    tiles_from(gathered, 1, work)
    up = dot(inv0_ref[...], work[...], 1, 1)
    up_ref[...] = up
    tiles_from(gathered, 2, work)
    work[...] = work[...] - dot(up, up, 0, 0)
    inv_ref[...] = factor(work, prev)


def last_kernel(ids, slab, own_rows, other_rows, x0, x1, inv0_ref, up_ref, inv1_ref, out_ref):
    row, col, depth = ids[0], ids[1], ids[2]
    rows_a, rows_b = wide_from(own_rows), wide_from(other_rows)
    rows0 = jnp.where(row == 0, rows_a, rows_b)
    rows1 = jnp.where(row == 0, rows_b, rows_a)
    row_id = lax.broadcasted_iota(jnp.int32, (2 * NB, NB), 0)
    tile_id = 4 * depth + 2 * (row_id // NB) + row
    inv0, up, inv1 = inv0_ref[...], up_ref[...], inv1_ref[...]
    p0 = dot(tile_from(x0), inv0, 1, 1)
    q0 = dot(inv0, rows0)
    b0 = jnp.where(tile_id > 0, p0, 0.0)
    p1 = jnp.where(tile_id >= 1, dot(tile_from(x1) - dot(b0, up), inv1, 1, 1), 0.0)
    q1 = dot(inv1, rows1 - dot(up, q0, 0, 0))
    b1 = jnp.where(tile_id > 1, p1, 0.0)
    change = dot(b0, q0) + dot(b1, q1)
    for q in range(4):
        piece = slab[pl.ds(q, 2 * NB, stride=4), :] - change[:, q * LANES : (q + 1) * LANES]
        if q < 2:
            lanes = slice(q * LANES, (q + 1) * LANES)
            piece = jnp.where(col == 0, p0[:, lanes], jnp.where(col == 1, p1[:, lanes], piece))
        out_ref[pl.ds(q, 2 * NB, stride=4), :] = piece


def whole(shape):
    return pl.BlockSpec(shape, lambda i, ids: (0,) * len(shape))


def call(kernel, ids, args, specs, outs, scratch, flops):
    return pl.pallas_call(
        kernel,
        out_shape=[jax.ShapeDtypeStruct(s, jnp.float32) for s in outs],
        grid_spec=pltpu.PrefetchScalarGridSpec(
            num_scalar_prefetch=1,
            grid=(1,),
            in_specs=specs,
            out_specs=[whole(s) for s in outs],
            scratch_shapes=[pltpu.VMEM(s, jnp.float32) for s in scratch],
        ),
        compiler_params=pltpu.CompilerParams(vmem_limit_bytes=32 * 1024 * 1024),
        cost_estimate=pl.CostEstimate(flops=flops, bytes_accessed=1 << 20, transcendentals=0),
    )(ids, *args)


def choose(col, table):
    out = table[0][0]
    for value, cols in table[1:]:
        for c in cols:
            out = jnp.where(col == c, value, out)
    return out


def shards(gram_slab):
    row = lax.axis_index("row")
    col = lax.axis_index("col")
    depth = lax.axis_index("depth")
    ids = jnp.stack([row, col, depth]).astype(jnp.int32)
    flat = gram_slab.reshape(32 * NB * 4, LANES)

    def swap(x):
        return lax.ppermute(x, "row", [(0, 1), (1, 0)])

    def send(x, pairs):
        return lax.ppermute(x, "col", pairs)

    def to_all(x, axis, size):
        return lax.all_to_all(jnp.broadcast_to(x[None], (size, *x.shape)), axis, 0, 0, tiled=True)

    tile = lax.dynamic_slice_in_dim(flat, depth * 64, 64, 0).reshape(16, 4, LANES)[:, :2]
    mine = to_all(tile.reshape(32, LANES), "col", 8)[:2]
    block = lax.dynamic_slice_in_dim(flat, depth * 2048, 2048, 0)
    strip = block.reshape(512, 4, LANES)[:, :2].reshape(1024, LANES)
    strip, mine = lax.optimization_barrier((strip, mine))
    x_a = send(strip, [(0, 3), (1, 4)])
    x_b = send(strip, [(0, 5), (1, 6)])
    other = swap(mine)
    upper, lower = jnp.where(row == 0, mine, other), jnp.where(row == 0, other, mine)
    gathered = to_all(jnp.stack([upper[0], lower[0], lower[1]]), "depth", 16)

    square = whole((NB, NB))
    scratch = [(NB, NB), (STEP, NB)]
    pieces = whole(gathered.shape)
    (inv0,) = call(first_kernel, ids, (gathered,), [pieces], [(NB, NB)], scratch, 10**10)
    x_a, x_b, inv0 = lax.optimization_barrier((x_a, x_b, inv0))
    held = choose(col, [(strip, ()), (x_a, (3, 4)), (x_b, (5, 6))])
    x_c = send(held, [(0, 1), (3, 4), (5, 6), (1, 2), (4, 5), (6, 7)])
    x_d = send(held, [(0, 7), (3, 2), (1, 0), (4, 3)])
    up, inv1 = call(
        second_kernel, ids, (gathered, inv0), [pieces, square], [(NB, NB)] * 2, scratch, 10**10
    )
    x0 = choose(col, [(held, ()), (x_c, (1, 4, 6)), (x_d, (2, 7))])
    x1 = choose(col, [(held, ()), (x_c, (2, 5, 7)), (x_d, (0, 3))])
    own_rows = flat[: NB * 4]
    other_rows = swap(own_rows)
    (out,) = call(
        last_kernel,
        ids,
        (block, own_rows, other_rows, x0, x1, inv0, up, inv1),
        [whole((2048, LANES))] + [whole((1024, LANES))] * 4 + [square] * 3,
        [(2048, LANES)],
        [],
        10**9,
    )
    return out.reshape(2, 1, NB, 2, 1, NB)


def solution(mesh):
    in_specs = (P(None, "row", None, None, "col", None),)
    out_specs = P("depth", "row", None, None, "col", None)
    return jax.shard_map(shards, mesh=mesh, in_specs=in_specs, out_specs=out_specs, check_vma=False)
```

```python
import jax
import jax.numpy as jnp
from jax import lax
from jax.experimental import pallas as pl
from jax.experimental.pallas import tpu as pltpu
from jax.sharding import PartitionSpec as P

NB = 256
STEP = 32
SUB = 8
LANES = 128
highest = lax.Precision.HIGHEST


def dot(a, b, ca=1, cb=0):
    return lax.dot_general(
        a, b, (((ca,), (cb,)), ((), ())), precision=highest, preferred_element_type=jnp.float32
    )


def thin_dot(a, b):
    def parts(x):
        first = x.astype(jnp.bfloat16)
        x = x - first.astype(jnp.float32)
        second = x.astype(jnp.bfloat16)
        third = (x - second.astype(jnp.float32)).astype(jnp.bfloat16)
        return first, second, third

    a1, a2, a3 = parts(a)
    b1, b2, b3 = parts(b)
    return lax.dot_general(
        jnp.concatenate([a1, a1, a2, a1, a2, a3], axis=0),
        jnp.concatenate([b1, b2, b1, b3, b2, b1], axis=0),
        (((0,), (0,)), ((), ())),
        preferred_element_type=jnp.float32,
    )


def tile_from(ref):
    rows = ref.shape[0] // 2
    return jnp.concatenate([ref[pl.ds(0, rows, stride=2), :], ref[pl.ds(1, rows, stride=2), :]], axis=1)


def wide_from(ref):
    rows = ref.shape[0] // 4
    return jnp.concatenate([ref[pl.ds(q, rows, stride=4), :] for q in range(4)], axis=1)


def factor_panel(panel):
    groups = STEP // SUB
    lo = [panel[SUB * g : SUB * (g + 1), :LANES] for g in range(groups)]
    hi = [panel[SUB * g : SUB * (g + 1), LANES:] for g in range(groups)]
    shape = (SUB, LANES)
    lane = lax.broadcasted_iota(jnp.int32, shape, 1)
    sub = lax.broadcasted_iota(jnp.int32, shape, 0)
    for q in range(groups):
        live = range(q, groups)
        cols = [
            {g: jnp.broadcast_to(lo[g][:, SUB * q + j : SUB * q + j + 1], shape) for g in live}
            for j in range(SUB)
        ]
        d = {(i, j): jnp.broadcast_to(cols[j][q][i : i + 1, :], shape) for j in range(SUB) for i in range(j, SUB)}
        scale, low, inv = [], {}, {}
        for j in range(SUB):
            s = lax.rsqrt(d[j, j])
            scale.append(s)
            for i in range(j + 1, SUB):
                low[i, j] = d[i, j] * s
            for k in range(j + 1, SUB):
                for i in range(k, SUB):
                    d[i, k] = d[i, k] - low[i, j] * low[k, j]
            inv[j, j] = s
            for k in range(j):
                total = low[j, k] * inv[k, k]
                for i in range(k + 1, j):
                    total = total + low[j, i] * inv[i, k]
                inv[j, k] = -(total * s)
        block = (lane >= SUB * q) & (lane < SUB * (q + 1))
        unit = jnp.where(lane == sub + SUB * q, 1.0, 0.0)
        row_lo = jnp.where(block, unit, lo[q])
        new_lo, new_hi = jnp.zeros(shape, jnp.float32), jnp.zeros(shape, jnp.float32)
        for j in range(SUB):
            weight = jnp.zeros(shape, jnp.float32)
            for i in range(j, SUB):
                weight = jnp.where(sub == i, inv[i, j], weight)
            new_lo = new_lo + weight * jnp.broadcast_to(row_lo[j : j + 1, :], shape)
            new_hi = new_hi + weight * jnp.broadcast_to(hi[q][j : j + 1, :], shape)
        lo[q], hi[q] = new_lo, new_hi
        below = range(q + 1, groups)
        for g in below:
            lo[g] = jnp.where(block, 0.0, lo[g])
        for j in range(SUB):
            u_lo = jnp.broadcast_to(lo[q][j : j + 1, :], shape)
            u_hi = jnp.broadcast_to(hi[q][j : j + 1, :], shape)
            for g in below:
                m = cols[j][g] * scale[j]
                for k in range(j + 1, SUB):
                    cols[k][g] = cols[k][g] - m * low[k, j]
                lo[g] = lo[g] - m * u_lo
                hi[g] = hi[g] - m * u_hi
    for g in range(groups):
        lo[g] = jnp.where((lane < STEP) & (lane > sub + SUB * g), 0.0, lo[g])
    return jnp.concatenate(
        [jnp.concatenate([lo[g], hi[g]], axis=1) for g in range(groups)], axis=0
    )


def factor(work, prev):
    row_id = lax.broadcasted_iota(jnp.int32, (NB, NB), 0)
    lane_id = lax.broadcasted_iota(jnp.int32, (NB, NB), 1)
    panel_lane = lax.broadcasted_iota(jnp.int32, (STEP, NB), 1)
    prev[...] = jnp.zeros((STEP, NB), jnp.float32)

    def body(step, carry):
        start = pl.multiple_of(step * STEP, STEP)
        stop = start + STEP
        turn = lax.rem(NB - start, NB)
        last = prev[...]
        rolled = pltpu.roll(last, turn, axis=1)
        panel = pltpu.roll(work[pl.ds(start, STEP), :], turn, axis=1)
        panel = jnp.where((panel_lane >= NB - STEP) & (step > 0), 0.0, panel)
        panel = panel - thin_dot(rolled[:, :STEP], rolled)
        panel = pltpu.roll(factor_panel(panel), start, axis=1)
        below = jnp.where(panel_lane >= stop, last, 0.0)
        spent = (row_id >= stop) & (lane_id >= start - STEP) & (lane_id < start)
        work[...] = jnp.where(spent, 0.0, work[...]) - thin_dot(below, last)
        work[pl.ds(start, STEP), :] = panel
        prev[...] = panel
        return carry

    lax.fori_loop(0, NB // STEP, body, 0)
    return jnp.where(lane_id <= row_id, work[...], 0.0)


def tiles_from(ids, pieces, k, out):
    y = ids[2] // 4
    for j in range(4):
        at = pl.multiple_of(lax.rem(y - j + 4, 4) * 64, 64)
        out[pl.ds(at, 64), :] = tile_from(pieces[j].at[k])


def first_tile(ref):
    return jnp.concatenate([ref[pl.ds(q, NB, stride=4), :] for q in range(2)], axis=1)


def first_kernel(ids, rows, out_ref, work, prev):
    @pl.when((ids[0] == 0) & (ids[1] == 0))
    def _():
        work[...] = first_tile(rows)
        inv = factor(work, prev)
        for q in range(2):
            out_ref[pl.ds(q, NB, stride=2), :] = inv[:, q * LANES : (q + 1) * LANES]


def second_kernel(ids, a, b, c, d, inv0_ref, up_ref, inv_ref, work, prev):
    pieces = (a, b, c, d)
    tiles_from(ids, pieces, 0, inv0_ref)
    tiles_from(ids, pieces, 1, work)
    up = dot(inv0_ref[...], work[...], 1, 1)
    up_ref[...] = up
    tiles_from(ids, pieces, 2, work)
    work[...] = work[...] - dot(up, up, 0, 0)
    inv_ref[...] = factor(work, prev)


def last_kernel(ids, slab, own_rows, other_rows, x0, x1, inv0_ref, up_ref, inv1_ref, out_ref):
    row, col, depth = ids[0], ids[1], ids[2]
    rows_a, rows_b = wide_from(own_rows), wide_from(other_rows)
    rows0 = jnp.where(row == 0, rows_a, rows_b)
    rows1 = jnp.where(row == 0, rows_b, rows_a)
    row_id = lax.broadcasted_iota(jnp.int32, (2 * NB, NB), 0)
    tile_id = 4 * depth + 2 * (row_id // NB) + row
    inv0, up, inv1 = inv0_ref[...], up_ref[...], inv1_ref[...]
    p0 = dot(tile_from(x0), inv0, 1, 1)
    q0 = dot(inv0, rows0)
    b0 = jnp.where(tile_id > 0, p0, 0.0)
    p1 = jnp.where(tile_id >= 1, dot(tile_from(x1) - dot(b0, up), inv1, 1, 1), 0.0)
    q1 = dot(inv1, rows1 - dot(up, q0, 0, 0))
    b1 = jnp.where(tile_id > 1, p1, 0.0)
    change = dot(b0, q0) + dot(b1, q1)
    for q in range(4):
        piece = slab[pl.ds(q, 2 * NB, stride=4), :] - change[:, q * LANES : (q + 1) * LANES]
        if q < 2:
            lanes = slice(q * LANES, (q + 1) * LANES)
            piece = jnp.where(col == 0, p0[:, lanes], jnp.where(col == 1, p1[:, lanes], piece))
        out_ref[pl.ds(q, 2 * NB, stride=4), :] = piece


def whole(shape):
    return pl.BlockSpec(shape, lambda i, ids: (0,) * len(shape))


def call(kernel, ids, args, specs, outs, scratch, flops):
    return pl.pallas_call(
        kernel,
        out_shape=[jax.ShapeDtypeStruct(s, jnp.float32) for s in outs],
        grid_spec=pltpu.PrefetchScalarGridSpec(
            num_scalar_prefetch=1,
            grid=(1,),
            in_specs=specs,
            out_specs=[whole(s) for s in outs],
            scratch_shapes=[pltpu.VMEM(s, jnp.float32) for s in scratch],
        ),
        compiler_params=pltpu.CompilerParams(vmem_limit_bytes=40 * 1024 * 1024),
        cost_estimate=pl.CostEstimate(flops=flops, bytes_accessed=1 << 20, transcendentals=0),
    )(ids, *args)


def choose(col, table):
    out = table[0][0]
    for value, cols in table[1:]:
        for c in cols:
            out = jnp.where(col == c, value, out)
    return out


def shards(gram_slab):
    row = lax.axis_index("row")
    col = lax.axis_index("col")
    depth = lax.axis_index("depth")
    ids = jnp.stack([row, col, depth]).astype(jnp.int32)
    flat = gram_slab.reshape(32 * NB * 4, LANES)

    def swap(x):
        return lax.ppermute(x, "row", [(0, 1), (1, 0)])

    def send(x, pairs):
        return lax.ppermute(x, "col", pairs)

    def far(x):
        return send(x, [(0, 3), (1, 4)]), send(x, [(0, 5), (1, 6)])

    def near(x):
        ahead = [(0, 1), (3, 4), (5, 6), (1, 2), (4, 5), (6, 7)]
        return send(x, ahead), send(x, [(0, 7), (3, 2), (1, 0), (4, 3)])

    def held_of(x, ahead, back):
        return choose(col, [(x, ()), (ahead, (3, 4)), (back, (5, 6))])

    def both_of(x, ahead, back):
        return (
            choose(col, [(x, ()), (ahead, (1, 4, 6)), (back, (2, 7))]),
            choose(col, [(x, ()), (ahead, (2, 5, 7)), (back, (0, 3))]),
        )

    square = whole((NB, NB))
    scratch = [(NB, NB), (STEP, NB)]
    first_rows = pl.BlockSpec((1024, LANES), lambda i, ids: (0, 0))
    (inv0,) = call(first_kernel, ids, (flat,), [first_rows], [(512, LANES)], scratch, 10**10)

    block = lax.dynamic_slice_in_dim(flat, depth * 2048, 2048, 0)
    strip = block.reshape(512, 4, LANES)[:, :2].reshape(1024, LANES)
    y = depth // 4
    tile = lax.dynamic_slice_in_dim(flat, y * 256, 256, 0).reshape(64, 4, LANES)[:, :2]
    inv0 = lax.dynamic_slice_in_dim(inv0, y * 128, 128, 0)
    tile = jnp.where((row == 0) & (col == 0), inv0, tile.reshape(128, LANES))
    x_a = send(strip, [(0, 5), (1, 4)])
    x_b = send(strip, [(0, 1), (1, 0)])
    tile = held_of(tile, *far(tile))
    tile, x_a, x_b = lax.optimization_barrier((tile, x_a, x_b))
    mine = jnp.stack(both_of(tile, *near(tile)))
    x_c = send(choose(col, [(x_a, ()), (x_b, (1,))]), [(1, 2), (5, 4), (4, 3)])
    x_d = send(choose(col, [(x_a, ()), (x_b, (0,))]), [(5, 6), (4, 5), (0, 7)])
    other = swap(mine)
    upper, lower = jnp.where(row == 0, mine, other), jnp.where(row == 0, other, mine)
    tiles = jnp.stack([upper[0], lower[0], lower[1]])
    pieces = [tiles] + [
        lax.ppermute(tiles, "depth", [(d, (d + 4 * j) % 16) for d in range(16)]) for j in (1, 2, 3)
    ]

    x_c, x_d, own_rows, *pieces = lax.optimization_barrier((x_c, x_d, flat[: NB * 4], *pieces))
    other_rows = swap(own_rows)
    x_e = send(choose(col, [(x_c, ()), (x_d, (5, 6))]), [(4, 3), (6, 7), (3, 2), (5, 6)])
    inv0, up, inv1 = call(
        second_kernel, ids, pieces, [whole(tiles.shape)] * 4, [(NB, NB)] * 3, scratch, 10**10
    )
    x_e, inv1 = lax.optimization_barrier((x_e, inv1))
    x0 = choose(col, [(x_e, ()), (strip, (0,)), (x_b, (1,)), (x_c, (2, 4)), (x_a, (5,)), (x_d, (6,))])
    x1 = choose(col, [(x_e, ()), (x_b, (0,)), (strip, (1,)), (x_c, (3,)), (x_a, (4,)), (x_d, (5, 7))])
    (out,) = call(
        last_kernel,
        ids,
        (block, own_rows, other_rows, x0, x1, inv0, up, inv1),
        [whole((2048, LANES))] + [whole((1024, LANES))] * 4 + [square] * 3,
        [(2048, LANES)],
        [],
        10**9,
    )
    return out.reshape(2, 1, NB, 2, 1, NB)


def solution(mesh):
    in_specs = (P(None, "row", None, None, "col", None),)
    out_specs = P("depth", "row", None, None, "col", None)
    return jax.shard_map(shards, mesh=mesh, in_specs=in_specs, out_specs=out_specs, check_vma=False)
```

```python
import jax
import jax.numpy as jnp
from jax import lax
from jax.experimental import pallas as pl
from jax.experimental.pallas import tpu as pltpu
from jax.sharding import PartitionSpec as P

NB = 256
STEP = 32
SUB = 8
LANES = 128
highest = lax.Precision.HIGHEST


def dot(a, b, ca=1, cb=0):
    return lax.dot_general(
        a, b, (((ca,), (cb,)), ((), ())), precision=highest, preferred_element_type=jnp.float32
    )


def thin_dot(a, b):
    def parts(x):
        first = x.astype(jnp.bfloat16)
        x = x - first.astype(jnp.float32)
        second = x.astype(jnp.bfloat16)
        third = (x - second.astype(jnp.float32)).astype(jnp.bfloat16)
        return first, second, third

    a1, a2, a3 = parts(a)
    b1, b2, b3 = parts(b)
    return lax.dot_general(
        jnp.concatenate([a1, a1, a2, a1, a2, a3], axis=0),
        jnp.concatenate([b1, b2, b1, b3, b2, b1], axis=0),
        (((0,), (0,)), ((), ())),
        preferred_element_type=jnp.float32,
    )


def tile_from(ref):
    rows = ref.shape[0] // 2
    return jnp.concatenate([ref[pl.ds(0, rows, stride=2), :], ref[pl.ds(1, rows, stride=2), :]], axis=1)


def wide_from(ref):
    rows = ref.shape[0] // 4
    return jnp.concatenate([ref[pl.ds(q, rows, stride=4), :] for q in range(4)], axis=1)


def factor_panel(panel):
    groups = STEP // SUB
    lo = [panel[SUB * g : SUB * (g + 1), :LANES] for g in range(groups)]
    hi = [panel[SUB * g : SUB * (g + 1), LANES:] for g in range(groups)]
    shape = (SUB, LANES)
    lane = lax.broadcasted_iota(jnp.int32, shape, 1)
    sub = lax.broadcasted_iota(jnp.int32, shape, 0)
    for q in range(groups):
        live = range(q, groups)
        cols = [
            {g: jnp.broadcast_to(lo[g][:, SUB * q + j : SUB * q + j + 1], shape) for g in live}
            for j in range(SUB)
        ]
        d = {(i, j): jnp.broadcast_to(cols[j][q][i : i + 1, :], shape) for j in range(SUB) for i in range(j, SUB)}
        scale, low, inv = [], {}, {}
        for j in range(SUB):
            s = lax.rsqrt(d[j, j])
            scale.append(s)
            for i in range(j + 1, SUB):
                low[i, j] = d[i, j] * s
            for k in range(j + 1, SUB):
                for i in range(k, SUB):
                    d[i, k] = d[i, k] - low[i, j] * low[k, j]
            inv[j, j] = s
            for k in range(j):
                total = low[j, k] * inv[k, k]
                for i in range(k + 1, j):
                    total = total + low[j, i] * inv[i, k]
                inv[j, k] = -(total * s)
        block = (lane >= SUB * q) & (lane < SUB * (q + 1))
        unit = jnp.where(lane == sub + SUB * q, 1.0, 0.0)
        row_lo = jnp.where(block, unit, lo[q])
        new_lo, new_hi = jnp.zeros(shape, jnp.float32), jnp.zeros(shape, jnp.float32)
        for j in range(SUB):
            weight = jnp.zeros(shape, jnp.float32)
            for i in range(j, SUB):
                weight = jnp.where(sub == i, inv[i, j], weight)
            new_lo = new_lo + weight * jnp.broadcast_to(row_lo[j : j + 1, :], shape)
            new_hi = new_hi + weight * jnp.broadcast_to(hi[q][j : j + 1, :], shape)
        lo[q], hi[q] = new_lo, new_hi
        below = range(q + 1, groups)
        for g in below:
            lo[g] = jnp.where(block, 0.0, lo[g])
        for j in range(SUB):
            u_lo = jnp.broadcast_to(lo[q][j : j + 1, :], shape)
            u_hi = jnp.broadcast_to(hi[q][j : j + 1, :], shape)
            for g in below:
                m = cols[j][g] * scale[j]
                for k in range(j + 1, SUB):
                    cols[k][g] = cols[k][g] - m * low[k, j]
                lo[g] = lo[g] - m * u_lo
                hi[g] = hi[g] - m * u_hi
    for g in range(groups):
        lo[g] = jnp.where((lane < STEP) & (lane > sub + SUB * g), 0.0, lo[g])
    return jnp.concatenate(
        [jnp.concatenate([lo[g], hi[g]], axis=1) for g in range(groups)], axis=0
    )


def factor(work, prev):
    row_id = lax.broadcasted_iota(jnp.int32, (NB, NB), 0)
    lane_id = lax.broadcasted_iota(jnp.int32, (NB, NB), 1)
    panel_lane = lax.broadcasted_iota(jnp.int32, (STEP, NB), 1)
    prev[...] = jnp.zeros((STEP, NB), jnp.float32)

    def body(step, carry):
        start = pl.multiple_of(step * STEP, STEP)
        stop = start + STEP
        turn = lax.rem(NB - start, NB)
        last = prev[...]
        rolled = pltpu.roll(last, turn, axis=1)
        panel = pltpu.roll(work[pl.ds(start, STEP), :], turn, axis=1)
        panel = jnp.where((panel_lane >= NB - STEP) & (step > 0), 0.0, panel)
        panel = panel - thin_dot(rolled[:, :STEP], rolled)
        panel = pltpu.roll(factor_panel(panel), start, axis=1)
        below = jnp.where(panel_lane >= stop, last, 0.0)
        spent = (row_id >= stop) & (lane_id >= start - STEP) & (lane_id < start)
        work[...] = jnp.where(spent, 0.0, work[...]) - thin_dot(below, last)
        work[pl.ds(start, STEP), :] = panel
        prev[...] = panel
        return carry

    lax.fori_loop(0, NB // STEP, body, 0)
    return jnp.where(lane_id <= row_id, work[...], 0.0)


def tiles_from(ids, pieces, k, out):
    y = ids[2] // 4
    for j in range(4):
        at = pl.multiple_of(lax.rem(y - j + 4, 4) * 64, 64)
        out[pl.ds(at, 64), :] = tile_from(pieces.at[j, k])


def first_tile(ref):
    return jnp.concatenate([ref[pl.ds(q, NB, stride=4), :] for q in range(2)], axis=1)


def first_kernel(ids, rows, out_ref, work, prev):
    @pl.when((ids[0] == 0) & (ids[1] == 0))
    def _():
        work[...] = first_tile(rows)
        inv = factor(work, prev)
        for q in range(2):
            out_ref[pl.ds(q, NB, stride=2), :] = inv[:, q * LANES : (q + 1) * LANES]


def second_kernel(ids, own, other, inv0_ref, up_ref, inv_ref, lower, work, prev):
    def place(upper, under):
        tiles_from(ids, upper, 0, inv0_ref)
        tiles_from(ids, under, 0, lower)
        tiles_from(ids, under, 1, work)

    pl.when(ids[0] == 0)(lambda: place(own, other))
    pl.when(ids[0] != 0)(lambda: place(other, own))
    up = dot(inv0_ref[...], lower[...], 1, 1)
    up_ref[...] = up
    work[...] = work[...] - dot(up, up, 0, 0)
    inv_ref[...] = factor(work, prev)


def last_kernel(ids, slab, own_rows, other_rows, x0, x1, inv0_ref, up_ref, inv1_ref, out_ref):
    row, col, depth = ids[0], ids[1], ids[2]
    rows_a, rows_b = wide_from(own_rows), wide_from(other_rows)
    rows0 = jnp.where(row == 0, rows_a, rows_b)
    rows1 = jnp.where(row == 0, rows_b, rows_a)
    row_id = lax.broadcasted_iota(jnp.int32, (2 * NB, NB), 0)
    tile_id = 4 * depth + 2 * (row_id // NB) + row
    inv0, up, inv1 = inv0_ref[...], up_ref[...], inv1_ref[...]
    p0 = dot(tile_from(x0), inv0, 1, 1)
    q0 = dot(inv0, rows0)
    b0 = jnp.where(tile_id > 0, p0, 0.0)
    p1 = jnp.where(tile_id >= 1, dot(tile_from(x1) - dot(b0, up), inv1, 1, 1), 0.0)
    q1 = dot(inv1, rows1 - dot(up, q0, 0, 0))
    b1 = jnp.where(tile_id > 1, p1, 0.0)
    change = dot(b0, q0) + dot(b1, q1)
    for q in range(4):
        piece = slab[pl.ds(q, 2 * NB, stride=4), :] - change[:, q * LANES : (q + 1) * LANES]
        if q < 2:
            lanes = slice(q * LANES, (q + 1) * LANES)
            piece = jnp.where(col == 0, p0[:, lanes], jnp.where(col == 1, p1[:, lanes], piece))
        out_ref[pl.ds(q, 2 * NB, stride=4), :] = piece


def whole(shape):
    return pl.BlockSpec(shape, lambda i, ids: (0,) * len(shape))


def call(kernel, ids, args, specs, outs, scratch, flops):
    return pl.pallas_call(
        kernel,
        out_shape=[jax.ShapeDtypeStruct(s, jnp.float32) for s in outs],
        grid_spec=pltpu.PrefetchScalarGridSpec(
            num_scalar_prefetch=1,
            grid=(1,),
            in_specs=specs,
            out_specs=[whole(s) for s in outs],
            scratch_shapes=[pltpu.VMEM(s, jnp.float32) for s in scratch],
        ),
        compiler_params=pltpu.CompilerParams(vmem_limit_bytes=40 * 1024 * 1024),
        cost_estimate=pl.CostEstimate(flops=flops, bytes_accessed=1 << 20, transcendentals=0),
    )(ids, *args)


def choose(col, table):
    out = table[0][0]
    for value, cols in table[1:]:
        for c in cols:
            out = jnp.where(col == c, value, out)
    return out


def shards(gram_slab):
    row = lax.axis_index("row")
    col = lax.axis_index("col")
    depth = lax.axis_index("depth")
    ids = jnp.stack([row, col, depth]).astype(jnp.int32)
    flat = gram_slab.reshape(32 * NB * 4, LANES)

    def swap(x):
        return lax.ppermute(x, "row", [(0, 1), (1, 0)])

    def send(x, pairs):
        return lax.ppermute(x, "col", pairs)

    def far(x):
        return send(x, [(0, 3), (1, 4)]), send(x, [(0, 5), (1, 6)])

    def near(x):
        ahead = [(0, 1), (3, 4), (5, 6), (1, 2), (4, 5), (6, 7)]
        return send(x, ahead), send(x, [(0, 7), (3, 2), (1, 0), (4, 3)])

    def held_of(x, ahead, back):
        return choose(col, [(x, ()), (ahead, (3, 4)), (back, (5, 6))])

    def both_of(x, ahead, back):
        return (
            choose(col, [(x, ()), (ahead, (1, 4, 6)), (back, (2, 7))]),
            choose(col, [(x, ()), (ahead, (2, 5, 7)), (back, (0, 3))]),
        )

    square = whole((NB, NB))
    scratch = [(NB, NB), (STEP, NB)]
    first_rows = pl.BlockSpec((1024, LANES), lambda i, ids: (0, 0))
    (inv0,) = call(first_kernel, ids, (flat,), [first_rows], [(512, LANES)], scratch, 10**10)

    strip = lax.dynamic_slice(gram_slab, (2 * depth, 0, 0, 0, 0, 0), (2, 1, NB, 1, 1, NB)).reshape(1024, LANES)
    y = depth // 4
    tile = lax.dynamic_slice_in_dim(flat, y * 256, 256, 0).reshape(64, 4, LANES)[:, :2]
    inv0 = lax.dynamic_slice_in_dim(inv0, y * 128, 128, 0)
    tile = jnp.where((row == 0) & (col == 0), inv0, tile.reshape(128, LANES))
    strip, tile = lax.optimization_barrier((strip, tile))
    x_b = send(strip, [(0, 1), (1, 0)])
    x_a = send(strip, [(0, 5), (1, 4)])
    tile = held_of(tile, *far(tile))
    mine = jnp.stack(both_of(tile, *near(tile)))
    mine, x_a, x_b = lax.optimization_barrier((mine, x_a, x_b))
    x_c = send(choose(col, [(x_a, ()), (x_b, (1,))]), [(1, 2), (5, 4), (4, 3)])
    x_d = send(choose(col, [(x_a, ()), (x_b, (0,))]), [(5, 6), (4, 5), (0, 7)])
    own = jnp.stack(
        [mine] + [lax.ppermute(mine, "depth", [(d, (d + 4 * j) % 16) for d in range(16)]) for j in (1, 2, 3)]
    )
    x_c, x_d, own = lax.optimization_barrier((x_c, x_d, own))
    other = swap(own)

    late_slab, own = lax.optimization_barrier((flat, own))
    block = lax.dynamic_slice_in_dim(late_slab, depth * 2048, 2048, 0)
    own_rows = late_slab[: NB * 4]
    own, other = lax.optimization_barrier((own, other))
    other_rows = swap(own_rows)
    x_e = send(choose(col, [(x_c, ()), (x_d, (5, 6))]), [(4, 3), (6, 7), (3, 2), (5, 6)])
    inv0, up, inv1 = call(
        second_kernel, ids, (own, other), [whole(own.shape)] * 2, [(NB, NB)] * 3, [(NB, NB)] + scratch, 10**10
    )
    x_e, inv1 = lax.optimization_barrier((x_e, inv1))
    x0 = choose(col, [(x_e, ()), (strip, (0,)), (x_b, (1,)), (x_c, (2, 4)), (x_a, (5,)), (x_d, (6,))])
    x1 = choose(col, [(x_e, ()), (x_b, (0,)), (strip, (1,)), (x_c, (3,)), (x_a, (4,)), (x_d, (5, 7))])
    (out,) = call(
        last_kernel,
        ids,
        (block, own_rows, other_rows, x0, x1, inv0, up, inv1),
        [whole((2048, LANES))] + [whole((1024, LANES))] * 4 + [square] * 3,
        [(2048, LANES)],
        [],
        10**9,
    )
    return out.reshape(2, 1, NB, 2, 1, NB)


def solution(mesh):
    in_specs = (P(None, "row", None, None, "col", None),)
    out_specs = P("depth", "row", None, None, "col", None)
    return jax.shard_map(shards, mesh=mesh, in_specs=in_specs, out_specs=out_specs, check_vma=False)
```

```python
import jax
import jax.numpy as jnp
from jax import lax
from jax.experimental import pallas as pl
from jax.experimental.pallas import tpu as pltpu
from jax.sharding import PartitionSpec as P

NB = 256
STEP = 64
SUB = 8
LANES = 128
highest = lax.Precision.HIGHEST


def dot(a, b, ca=1, cb=0):
    return lax.dot_general(
        a, b, (((ca,), (cb,)), ((), ())), precision=highest, preferred_element_type=jnp.float32
    )


def thin_dot(a, b):
    def parts(x):
        first = x.astype(jnp.bfloat16)
        x = x - first.astype(jnp.float32)
        second = x.astype(jnp.bfloat16)
        third = (x - second.astype(jnp.float32)).astype(jnp.bfloat16)
        return first, second, third

    a1, a2, a3 = parts(a)
    b1, b2, b3 = parts(b)
    return lax.dot_general(
        jnp.concatenate([a1, a1, a2, a1, a2, a3], axis=0),
        jnp.concatenate([b1, b2, b1, b3, b2, b1], axis=0),
        (((0,), (0,)), ((), ())),
        preferred_element_type=jnp.float32,
    )


def tile_from(ref):
    rows = ref.shape[0] // 2
    return jnp.concatenate([ref[pl.ds(0, rows, stride=2), :], ref[pl.ds(1, rows, stride=2), :]], axis=1)


def wide_from(ref):
    rows = ref.shape[0] // 4
    return jnp.concatenate([ref[pl.ds(q, rows, stride=4), :] for q in range(4)], axis=1)


def factor_panel(panel):
    groups = STEP // SUB
    lo = [panel[SUB * g : SUB * (g + 1), :LANES] for g in range(groups)]
    hi = [panel[SUB * g : SUB * (g + 1), LANES:] for g in range(groups)]
    shape = (SUB, LANES)
    lane = lax.broadcasted_iota(jnp.int32, shape, 1)
    sub = lax.broadcasted_iota(jnp.int32, shape, 0)
    for q in range(groups):
        live = range(q, groups)
        cols = [
            {g: jnp.broadcast_to(lo[g][:, SUB * q + j : SUB * q + j + 1], shape) for g in live}
            for j in range(SUB)
        ]
        d = {(i, j): jnp.broadcast_to(cols[j][q][i : i + 1, :], shape) for j in range(SUB) for i in range(j, SUB)}
        scale, low, inv = [], {}, {}
        for j in range(SUB):
            s = lax.rsqrt(d[j, j])
            scale.append(s)
            for i in range(j + 1, SUB):
                low[i, j] = d[i, j] * s
            for k in range(j + 1, SUB):
                for i in range(k, SUB):
                    d[i, k] = d[i, k] - low[i, j] * low[k, j]
            inv[j, j] = s
            for k in range(j):
                total = low[j, k] * inv[k, k]
                for i in range(k + 1, j):
                    total = total + low[j, i] * inv[i, k]
                inv[j, k] = -(total * s)
        block = (lane >= SUB * q) & (lane < SUB * (q + 1))
        unit = jnp.where(lane == sub + SUB * q, 1.0, 0.0)
        row_lo = jnp.where(block, unit, lo[q])
        new_lo, new_hi = jnp.zeros(shape, jnp.float32), jnp.zeros(shape, jnp.float32)
        for j in range(SUB):
            weight = jnp.zeros(shape, jnp.float32)
            for i in range(j, SUB):
                weight = jnp.where(sub == i, inv[i, j], weight)
            new_lo = new_lo + weight * jnp.broadcast_to(row_lo[j : j + 1, :], shape)
            new_hi = new_hi + weight * jnp.broadcast_to(hi[q][j : j + 1, :], shape)
        lo[q], hi[q] = new_lo, new_hi
        below = range(q + 1, groups)
        for g in below:
            lo[g] = jnp.where(block, 0.0, lo[g])
        for j in range(SUB):
            u_lo = jnp.broadcast_to(lo[q][j : j + 1, :], shape)
            u_hi = jnp.broadcast_to(hi[q][j : j + 1, :], shape)
            for g in below:
                m = cols[j][g] * scale[j]
                for k in range(j + 1, SUB):
                    cols[k][g] = cols[k][g] - m * low[k, j]
                lo[g] = lo[g] - m * u_lo
                hi[g] = hi[g] - m * u_hi
    for g in range(groups):
        lo[g] = jnp.where((lane < STEP) & (lane > sub + SUB * g), 0.0, lo[g])
    return jnp.concatenate(
        [jnp.concatenate([lo[g], hi[g]], axis=1) for g in range(groups)], axis=0
    )


def factor(work, prev):
    row_id = lax.broadcasted_iota(jnp.int32, (NB, NB), 0)
    lane_id = lax.broadcasted_iota(jnp.int32, (NB, NB), 1)
    panel_lane = lax.broadcasted_iota(jnp.int32, (STEP, NB), 1)
    prev[...] = jnp.zeros((STEP, NB), jnp.float32)

    def body(step, carry):
        start = pl.multiple_of(step * STEP, STEP)
        stop = start + STEP
        turn = lax.rem(NB - start, NB)
        last = prev[...]
        rolled = pltpu.roll(last, turn, axis=1)
        panel = pltpu.roll(work[pl.ds(start, STEP), :], turn, axis=1)
        panel = jnp.where((panel_lane >= NB - STEP) & (step > 0), 0.0, panel)
        panel = panel - thin_dot(rolled[:, :STEP], rolled)
        panel = pltpu.roll(factor_panel(panel), start, axis=1)
        below = jnp.where(panel_lane >= stop, last, 0.0)
        spent = (row_id >= stop) & (lane_id >= start - STEP) & (lane_id < start)
        work[...] = jnp.where(spent, 0.0, work[...]) - thin_dot(below, last)
        work[pl.ds(start, STEP), :] = panel
        prev[...] = panel
        return carry

    lax.fori_loop(0, NB // STEP, body, 0)
    return jnp.where(lane_id <= row_id, work[...], 0.0)


def tiles_from(ids, pieces, k, out):
    y = ids[2] // 4
    for j in range(4):
        at = pl.multiple_of(lax.rem(y - j + 4, 4) * 64, 64)
        out[pl.ds(at, 64), :] = tile_from(pieces.at[j, k])


def first_tile(ref):
    return jnp.concatenate([ref[pl.ds(q, NB, stride=4), :] for q in range(2)], axis=1)


def first_kernel(ids, flat, inv_ref, rows_ref, slab_ref, work, prev, sems):
    rows = pltpu.make_async_copy(flat.at[pl.ds(0, 4 * NB), :], rows_ref, sems.at[0])
    start = pl.multiple_of(ids[2] * 8 * NB, 8 * NB)
    slab = pltpu.make_async_copy(flat.at[pl.ds(start, 8 * NB), :], slab_ref, sems.at[1])
    rows.start()
    slab.start()
    rows.wait()

    @pl.when((ids[0] == 0) & (ids[1] == 0))
    def _():
        work[...] = first_tile(rows_ref)
        inv = factor(work, prev)
        for q in range(2):
            inv_ref[pl.ds(q, NB, stride=2), :] = inv[:, q * LANES : (q + 1) * LANES]

    slab.wait()


def second_kernel(ids, own, other, inv0_ref, up_ref, inv_ref, lower, work, prev):
    def place(upper, under):
        tiles_from(ids, upper, 0, inv0_ref)
        tiles_from(ids, under, 0, lower)
        tiles_from(ids, under, 1, work)

    pl.when(ids[0] == 0)(lambda: place(own, other))
    pl.when(ids[0] != 0)(lambda: place(other, own))
    up = dot(inv0_ref[...], lower[...], 1, 1)
    up_ref[...] = up
    work[...] = work[...] - dot(up, up, 0, 0)
    inv_ref[...] = factor(work, prev)


def last_kernel(ids, slab, own_rows, other_rows, x0, x1, inv0_ref, up_ref, inv1_ref, out_ref):
    row, col, depth = ids[0], ids[1], ids[2]
    rows_a, rows_b = wide_from(own_rows), wide_from(other_rows)
    rows0 = jnp.where(row == 0, rows_a, rows_b)
    rows1 = jnp.where(row == 0, rows_b, rows_a)
    row_id = lax.broadcasted_iota(jnp.int32, (2 * NB, NB), 0)
    tile_id = 4 * depth + 2 * (row_id // NB) + row
    inv0, up, inv1 = inv0_ref[...], up_ref[...], inv1_ref[...]
    p0 = dot(tile_from(x0), inv0, 1, 1)
    q0 = dot(inv0, rows0)
    b0 = jnp.where(tile_id > 0, p0, 0.0)
    p1 = jnp.where(tile_id >= 1, dot(tile_from(x1) - dot(b0, up), inv1, 1, 1), 0.0)
    q1 = dot(inv1, rows1 - dot(up, q0, 0, 0))
    b1 = jnp.where(tile_id > 1, p1, 0.0)
    change = dot(b0, q0) + dot(b1, q1)
    for q in range(4):
        piece = slab[pl.ds(q, 2 * NB, stride=4), :] - change[:, q * LANES : (q + 1) * LANES]
        if q < 2:
            lanes = slice(q * LANES, (q + 1) * LANES)
            piece = jnp.where(col == 0, p0[:, lanes], jnp.where(col == 1, p1[:, lanes], piece))
        out_ref[pl.ds(q, 2 * NB, stride=4), :] = piece


def whole(shape):
    return pl.BlockSpec(shape, lambda i, ids: (0,) * len(shape))


def call(kernel, ids, args, specs, outs, scratch, flops, vmem):
    return pl.pallas_call(
        kernel,
        out_shape=[jax.ShapeDtypeStruct(s, jnp.float32) for s in outs],
        grid_spec=pltpu.PrefetchScalarGridSpec(
            num_scalar_prefetch=1,
            grid=(1,),
            in_specs=specs,
            out_specs=[whole(s) for s in outs],
            scratch_shapes=scratch,
        ),
        compiler_params=pltpu.CompilerParams(vmem_limit_bytes=vmem << 20),
        cost_estimate=pl.CostEstimate(flops=flops, bytes_accessed=1 << 20, transcendentals=0),
    )(ids, *args)


def choose(col, table):
    out = table[0][0]
    for value, cols in table[1:]:
        for c in cols:
            out = jnp.where(col == c, value, out)
    return out


def shards(gram_slab):
    row = lax.axis_index("row")
    col = lax.axis_index("col")
    depth = lax.axis_index("depth")
    ids = jnp.stack([row, col, depth]).astype(jnp.int32)
    flat = gram_slab.reshape(32 * NB * 4, LANES)

    def swap(x):
        return lax.ppermute(x, "row", [(0, 1), (1, 0)])

    def send(x, pairs):
        return lax.ppermute(x, "col", pairs)

    def far(x):
        return send(x, [(0, 3), (1, 4)]), send(x, [(0, 5), (1, 6)])

    def near(x):
        ahead = [(0, 1), (3, 4), (5, 6), (1, 2), (4, 5), (6, 7)]
        return send(x, ahead), send(x, [(0, 7), (3, 2), (1, 0), (4, 3)])

    def held_of(x, ahead, back):
        return choose(col, [(x, ()), (ahead, (3, 4)), (back, (5, 6))])

    def both_of(x, ahead, back):
        return (
            choose(col, [(x, ()), (ahead, (1, 4, 6)), (back, (2, 7))]),
            choose(col, [(x, ()), (ahead, (2, 5, 7)), (back, (0, 3))]),
        )

    square = whole((NB, NB))
    scratch = [pltpu.VMEM((NB, NB), jnp.float32), pltpu.VMEM((STEP, NB), jnp.float32)]
    inv0, own_rows, block = call(
        first_kernel,
        ids,
        (flat,),
        [pl.BlockSpec(memory_space=pl.ANY)],
        [(512, LANES), (1024, LANES), (2048, LANES)],
        scratch + [pltpu.SemaphoreType.DMA((2,))],
        10**10,
        40,
    )

    strip = block.reshape(512, 4, LANES)[:, :2].reshape(1024, LANES)
    y = depth // 4
    tile = lax.dynamic_slice_in_dim(own_rows, y * 256, 256, 0).reshape(64, 4, LANES)[:, :2]
    inv0 = lax.dynamic_slice_in_dim(inv0, y * 128, 128, 0)
    tile = jnp.where((row == 0) & (col == 0), inv0, tile.reshape(128, LANES))
    strip, tile = lax.optimization_barrier((strip, tile))
    x_a = send(strip, [(0, 5), (1, 4)])
    x_b = send(strip, [(0, 1), (1, 0)])
    tile = held_of(tile, *far(tile))
    mine = jnp.stack(both_of(tile, *near(tile)))
    x_b, x_a, mine = lax.optimization_barrier((x_b, x_a, mine))
    x_c = send(choose(col, [(x_a, ()), (x_b, (1,))]), [(1, 2), (5, 4), (4, 3)])
    x_d = send(choose(col, [(x_a, ()), (x_b, (0,))]), [(5, 6), (4, 5), (0, 7)])
    own = jnp.stack(
        [mine] + [lax.ppermute(mine, "depth", [(d, (d + 4 * j) % 16) for d in range(16)]) for j in (1, 2, 3)]
    )
    x_c, x_d, own = lax.optimization_barrier((x_c, x_d, own))
    other = swap(own)

    own, other, own_rows = lax.optimization_barrier((own, other, own_rows))
    other_rows = swap(own_rows)
    x_e = send(choose(col, [(x_c, ()), (x_d, (5, 6))]), [(4, 3), (6, 7), (3, 2), (5, 6)])
    inv0, up, inv1 = call(
        second_kernel, ids, (own, other), [whole(own.shape)] * 2, [(NB, NB)] * 3, scratch[:1] + scratch, 10**10, 12
    )
    x_e, inv1 = lax.optimization_barrier((x_e, inv1))
    x0 = choose(col, [(x_e, ()), (strip, (0,)), (x_b, (1,)), (x_c, (2, 4)), (x_a, (5,)), (x_d, (6,))])
    x1 = choose(col, [(x_e, ()), (x_b, (0,)), (strip, (1,)), (x_c, (3,)), (x_a, (4,)), (x_d, (5, 7))])
    (out,) = call(
        last_kernel,
        ids,
        (block, own_rows, other_rows, x0, x1, inv0, up, inv1),
        [whole((2048, LANES))] + [whole((1024, LANES))] * 4 + [square] * 3,
        [(2048, LANES)],
        [],
        10**9,
        32,
    )
    return out.reshape(2, 1, NB, 2, 1, NB)


def solution(mesh):
    in_specs = (P(None, "row", None, None, "col", None),)
    out_specs = P("depth", "row", None, None, "col", None)
    return jax.shard_map(shards, mesh=mesh, in_specs=in_specs, out_specs=out_specs, check_vma=False)
```

```python
import jax
import jax.numpy as jnp
from jax import lax
from jax.experimental import pallas as pl
from jax.experimental.pallas import tpu as pltpu
from jax.sharding import PartitionSpec as P

NB = 256
STEP = 64
SUB = 8
LANES = 128
highest = lax.Precision.HIGHEST


def dot(a, b, ca=1, cb=0):
    return lax.dot_general(
        a, b, (((ca,), (cb,)), ((), ())), precision=highest, preferred_element_type=jnp.float32
    )


def thin_dot(a, b):
    def parts(x):
        first = x.astype(jnp.bfloat16)
        x = x - first.astype(jnp.float32)
        second = x.astype(jnp.bfloat16)
        third = (x - second.astype(jnp.float32)).astype(jnp.bfloat16)
        return first, second, third

    a1, a2, a3 = parts(a)
    b1, b2, b3 = parts(b)
    return lax.dot_general(
        jnp.concatenate([a1, a1, a2, a1, a2, a3], axis=0),
        jnp.concatenate([b1, b2, b1, b3, b2, b1], axis=0),
        (((0,), (0,)), ((), ())),
        preferred_element_type=jnp.float32,
    )


def tile_from(ref):
    rows = ref.shape[0] // 2
    return jnp.concatenate([ref[pl.ds(0, rows, stride=2), :], ref[pl.ds(1, rows, stride=2), :]], axis=1)


def wide_from(ref):
    rows = ref.shape[0] // 4
    return jnp.concatenate([ref[pl.ds(q, rows, stride=4), :] for q in range(4)], axis=1)


def factor_panel(panel):
    groups = STEP // SUB
    lo = [panel[SUB * g : SUB * (g + 1), :LANES] for g in range(groups)]
    hi = [panel[SUB * g : SUB * (g + 1), LANES:] for g in range(groups)]
    shape = (SUB, LANES)
    lane = lax.broadcasted_iota(jnp.int32, shape, 1)
    sub = lax.broadcasted_iota(jnp.int32, shape, 0)
    for q in range(groups):
        live = range(q, groups)
        cols = [
            {g: jnp.broadcast_to(lo[g][:, SUB * q + j : SUB * q + j + 1], shape) for g in live}
            for j in range(SUB)
        ]
        d = {(i, j): jnp.broadcast_to(cols[j][q][i : i + 1, :], shape) for j in range(SUB) for i in range(j, SUB)}
        scale, low, inv = [], {}, {}
        for j in range(SUB):
            s = lax.rsqrt(d[j, j])
            scale.append(s)
            for i in range(j + 1, SUB):
                low[i, j] = d[i, j] * s
            for k in range(j + 1, SUB):
                for i in range(k, SUB):
                    d[i, k] = d[i, k] - low[i, j] * low[k, j]
            inv[j, j] = s
            for k in range(j):
                total = low[j, k] * inv[k, k]
                for i in range(k + 1, j):
                    total = total + low[j, i] * inv[i, k]
                inv[j, k] = -(total * s)
        block = (lane >= SUB * q) & (lane < SUB * (q + 1))
        unit = jnp.where(lane == sub + SUB * q, 1.0, 0.0)
        row_lo = jnp.where(block, unit, lo[q])
        new_lo, new_hi = jnp.zeros(shape, jnp.float32), jnp.zeros(shape, jnp.float32)
        for j in range(SUB):
            weight = jnp.zeros(shape, jnp.float32)
            for i in range(j, SUB):
                weight = jnp.where(sub == i, inv[i, j], weight)
            new_lo = new_lo + weight * jnp.broadcast_to(row_lo[j : j + 1, :], shape)
            new_hi = new_hi + weight * jnp.broadcast_to(hi[q][j : j + 1, :], shape)
        lo[q], hi[q] = new_lo, new_hi
        below = range(q + 1, groups)
        for g in below:
            lo[g] = jnp.where(block, 0.0, lo[g])
        for j in range(SUB):
            u_lo = jnp.broadcast_to(lo[q][j : j + 1, :], shape)
            u_hi = jnp.broadcast_to(hi[q][j : j + 1, :], shape)
            for g in below:
                m = cols[j][g] * scale[j]
                for k in range(j + 1, SUB):
                    cols[k][g] = cols[k][g] - m * low[k, j]
                lo[g] = lo[g] - m * u_lo
                hi[g] = hi[g] - m * u_hi
    for g in range(groups):
        lo[g] = jnp.where((lane < STEP) & (lane > sub + SUB * g), 0.0, lo[g])
    return jnp.concatenate(
        [jnp.concatenate([lo[g], hi[g]], axis=1) for g in range(groups)], axis=0
    )


def factor(work, prev):
    row_id = lax.broadcasted_iota(jnp.int32, (NB, NB), 0)
    lane_id = lax.broadcasted_iota(jnp.int32, (NB, NB), 1)
    panel_lane = lax.broadcasted_iota(jnp.int32, (STEP, NB), 1)
    prev[...] = jnp.zeros((STEP, NB), jnp.float32)

    def body(step, carry):
        start = pl.multiple_of(step * STEP, STEP)
        stop = start + STEP
        turn = lax.rem(NB - start, NB)
        last = prev[...]
        rolled = pltpu.roll(last, turn, axis=1)
        panel = pltpu.roll(work[pl.ds(start, STEP), :], turn, axis=1)
        panel = jnp.where((panel_lane >= NB - STEP) & (step > 0), 0.0, panel)
        panel = panel - thin_dot(rolled[:, :STEP], rolled)
        panel = pltpu.roll(factor_panel(panel), start, axis=1)
        below = jnp.where(panel_lane >= stop, last, 0.0)
        spent = (row_id >= stop) & (lane_id >= start - STEP) & (lane_id < start)
        work[...] = jnp.where(spent, 0.0, work[...]) - thin_dot(below, last)
        work[pl.ds(start, STEP), :] = panel
        prev[...] = panel
        return carry

    lax.fori_loop(0, NB // STEP, body, 0)
    return jnp.where(lane_id <= row_id, work[...], 0.0)


def tiles_from(ids, pieces, k, out):
    y = ids[2] // 4
    for j in range(4):
        at = pl.multiple_of(lax.rem(y - j + 4, 4) * 64, 64)
        out[pl.ds(at, 64), :] = tile_from(pieces.at[j, k])


def first_tile(ref):
    return jnp.concatenate([ref[pl.ds(q, NB, stride=4), :] for q in range(2)], axis=1)


def first_kernel(ids, flat, inv_ref, rows_ref, slab_ref, work, prev, sems):
    rows = pltpu.make_async_copy(flat.at[pl.ds(0, 4 * NB), :], rows_ref, sems.at[0])
    start = pl.multiple_of(ids[2] * 8 * NB, 8 * NB)
    slab = pltpu.make_async_copy(flat.at[pl.ds(start, 8 * NB), :], slab_ref, sems.at[1])
    rows.start()
    slab.start()
    rows.wait()

    @pl.when((ids[0] == 0) & (ids[1] == 0))
    def _():
        work[...] = first_tile(rows_ref)
        inv = factor(work, prev)
        for q in range(2):
            inv_ref[pl.ds(q, NB, stride=2), :] = inv[:, q * LANES : (q + 1) * LANES]

    slab.wait()


def second_kernel(ids, own, other, inv0_ref, up_ref, inv_ref, lower, work, prev):
    def place(upper, under):
        tiles_from(ids, upper, 0, inv0_ref)
        tiles_from(ids, under, 0, lower)
        tiles_from(ids, under, 1, work)

    pl.when(ids[0] == 0)(lambda: place(own, other))
    pl.when(ids[0] != 0)(lambda: place(other, own))
    up = dot(inv0_ref[...], lower[...], 1, 1)
    up_ref[...] = up
    work[...] = work[...] - dot(up, up, 0, 0)
    inv_ref[...] = factor(work, prev)


def last_kernel(ids, slab, own_rows, other_rows, x0, x1, inv0_ref, up_ref, inv1_ref, out_ref):
    row, col, depth = ids[0], ids[1], ids[2]
    rows_a, rows_b = wide_from(own_rows), wide_from(other_rows)
    rows0 = jnp.where(row == 0, rows_a, rows_b)
    rows1 = jnp.where(row == 0, rows_b, rows_a)
    row_id = lax.broadcasted_iota(jnp.int32, (2 * NB, NB), 0)
    tile_id = 4 * depth + 2 * (row_id // NB) + row
    inv0, up, inv1 = inv0_ref[...], up_ref[...], inv1_ref[...]
    p0 = dot(tile_from(x0), inv0, 1, 1)
    q0 = dot(inv0, rows0)
    b0 = jnp.where(tile_id > 0, p0, 0.0)
    p1 = jnp.where(tile_id >= 1, dot(tile_from(x1) - dot(b0, up), inv1, 1, 1), 0.0)
    q1 = dot(inv1, rows1 - dot(up, q0, 0, 0))
    b1 = jnp.where(tile_id > 1, p1, 0.0)
    change = dot(b0, q0) + dot(b1, q1)
    for q in range(4):
        piece = slab[pl.ds(q, 2 * NB, stride=4), :] - change[:, q * LANES : (q + 1) * LANES]
        if q < 2:
            lanes = slice(q * LANES, (q + 1) * LANES)
            piece = jnp.where(col == 0, p0[:, lanes], jnp.where(col == 1, p1[:, lanes], piece))
        out_ref[pl.ds(q, 2 * NB, stride=4), :] = piece


def whole(shape):
    return pl.BlockSpec(shape, lambda i, ids: (0,) * len(shape))


def call(kernel, ids, args, specs, outs, scratch, flops, vmem):
    return pl.pallas_call(
        kernel,
        out_shape=[jax.ShapeDtypeStruct(s, jnp.float32) for s in outs],
        grid_spec=pltpu.PrefetchScalarGridSpec(
            num_scalar_prefetch=1,
            grid=(1,),
            in_specs=specs,
            out_specs=[whole(s) for s in outs],
            scratch_shapes=scratch,
        ),
        compiler_params=pltpu.CompilerParams(vmem_limit_bytes=vmem << 20),
        cost_estimate=pl.CostEstimate(flops=flops, bytes_accessed=1 << 20, transcendentals=0),
    )(ids, *args)


def choose(col, table):
    out = table[0][0]
    for value, cols in table[1:]:
        for c in cols:
            out = jnp.where(col == c, value, out)
    return out


def shards(gram_slab):
    row = lax.axis_index("row")
    col = lax.axis_index("col")
    depth = lax.axis_index("depth")
    ids = jnp.stack([row, col, depth]).astype(jnp.int32)
    flat = gram_slab.reshape(32 * NB * 4, LANES)

    def swap(x):
        return lax.ppermute(x, "row", [(0, 1), (1, 0)])

    def send(x, pairs):
        return lax.ppermute(x, "col", pairs)

    def far(x):
        return send(x, [(0, 3), (1, 4)]), send(x, [(0, 5), (1, 6)])

    def near(x):
        ahead = [(0, 1), (3, 4), (5, 6), (1, 2), (4, 5), (6, 7)]
        return send(x, ahead), send(x, [(0, 7), (3, 2), (1, 0), (4, 3)])

    def held_of(x, ahead, back):
        return choose(col, [(x, ()), (ahead, (3, 4)), (back, (5, 6))])

    def both_of(x, ahead, back):
        return (
            choose(col, [(x, ()), (ahead, (1, 4, 6)), (back, (2, 7))]),
            choose(col, [(x, ()), (ahead, (2, 5, 7)), (back, (0, 3))]),
        )

    square = whole((NB, NB))
    scratch = [pltpu.VMEM((NB, NB), jnp.float32), pltpu.VMEM((STEP, NB), jnp.float32)]
    inv0, own_rows, block = call(
        first_kernel,
        ids,
        (flat,),
        [pl.BlockSpec(memory_space=pl.ANY)],
        [(512, LANES), (1024, LANES), (2048, LANES)],
        scratch + [pltpu.SemaphoreType.DMA((2,))],
        10**10,
        40,
    )

    strip = block.reshape(512, 4, LANES)[:, :2].reshape(1024, LANES)
    y = depth // 4
    tile = lax.dynamic_slice_in_dim(own_rows, y * 256, 256, 0).reshape(64, 4, LANES)[:, :2]
    inv0 = lax.dynamic_slice_in_dim(inv0, y * 128, 128, 0)
    tile = jnp.where((row == 0) & (col == 0), inv0, tile.reshape(128, LANES))
    strip, tile = lax.optimization_barrier((strip, tile))
    x_a = send(strip, [(0, 5), (1, 4)])
    tile = held_of(tile, *far(tile))
    mine = jnp.stack(both_of(tile, *near(tile)))
    x_a, mine = lax.optimization_barrier((x_a, mine))
    held = choose(col, [(x_a, ()), (strip, (0, 1))])
    x_b = send(held, [(0, 1), (5, 4), (4, 3)])
    x_c = send(held, [(1, 0), (5, 6), (4, 5)])
    own = jnp.stack(
        [mine] + [lax.ppermute(mine, "depth", [(d, (d + 4 * j) % 16) for d in range(16)]) for j in (1, 2, 3)]
    )
    x_b, x_c, own = lax.optimization_barrier((x_b, x_c, own))
    other = swap(own)

    own, other, own_rows = lax.optimization_barrier((own, other, own_rows))
    other_rows = swap(own_rows)
    held = choose(col, [(x_b, ()), (x_c, (0, 5, 6))])
    x_d = send(held, [(4, 3), (6, 7), (3, 2), (5, 6)])
    x_e = send(held, [(1, 2), (0, 7)])
    inv0, up, inv1 = call(
        second_kernel, ids, (own, other), [whole(own.shape)] * 2, [(NB, NB)] * 3, scratch[:1] + scratch, 10**10, 12
    )
    x_d, x_e, inv1 = lax.optimization_barrier((x_d, x_e, inv1))
    x0 = choose(col, [(x_d, ()), (strip, (0,)), (x_b, (1, 4)), (x_e, (2,)), (x_a, (5,)), (x_c, (6,))])
    x1 = choose(col, [(x_d, ()), (x_c, (0, 5)), (strip, (1,)), (x_b, (3,)), (x_a, (4,)), (x_e, (7,))])
    (out,) = call(
        last_kernel,
        ids,
        (block, own_rows, other_rows, x0, x1, inv0, up, inv1),
        [whole((2048, LANES))] + [whole((1024, LANES))] * 4 + [square] * 3,
        [(2048, LANES)],
        [],
        10**9,
        32,
    )
    return out.reshape(2, 1, NB, 2, 1, NB)


def solution(mesh):
    in_specs = (P(None, "row", None, None, "col", None),)
    out_specs = P("depth", "row", None, None, "col", None)
    return jax.shard_map(shards, mesh=mesh, in_specs=in_specs, out_specs=out_specs, check_vma=False)
```

```python
import jax
import jax.numpy as jnp
from jax import lax
from jax.experimental import pallas as pl
from jax.experimental.pallas import tpu as pltpu
from jax.sharding import PartitionSpec as P

NB = 256
STEP = 64
SUB = 8
LANES = 128
highest = lax.Precision.HIGHEST


def dot(a, b, ca=1, cb=0):
    return lax.dot_general(
        a, b, (((ca,), (cb,)), ((), ())), precision=highest, preferred_element_type=jnp.float32
    )


def thin_dot(a, b):
    def parts(x):
        first = x.astype(jnp.bfloat16)
        x = x - first.astype(jnp.float32)
        second = x.astype(jnp.bfloat16)
        third = (x - second.astype(jnp.float32)).astype(jnp.bfloat16)
        return first, second, third

    a1, a2, a3 = parts(a)
    b1, b2, b3 = parts(b)
    return lax.dot_general(
        jnp.concatenate([a1, a1, a2, a1, a2, a3], axis=0),
        jnp.concatenate([b1, b2, b1, b3, b2, b1], axis=0),
        (((0,), (0,)), ((), ())),
        preferred_element_type=jnp.float32,
    )


def tile_from(ref):
    rows = ref.shape[0] // 2
    return jnp.concatenate([ref[pl.ds(0, rows, stride=2), :], ref[pl.ds(1, rows, stride=2), :]], axis=1)


def wide_from(ref):
    rows = ref.shape[0] // 4
    return jnp.concatenate([ref[pl.ds(q, rows, stride=4), :] for q in range(4)], axis=1)


def factor_panel(panel):
    groups = STEP // SUB
    lo = [panel[SUB * g : SUB * (g + 1), :LANES] for g in range(groups)]
    hi = [panel[SUB * g : SUB * (g + 1), LANES:] for g in range(groups)]
    shape = (SUB, LANES)
    lane = lax.broadcasted_iota(jnp.int32, shape, 1)
    sub = lax.broadcasted_iota(jnp.int32, shape, 0)
    for q in range(groups):
        live = range(q, groups)
        cols = [
            {g: jnp.broadcast_to(lo[g][:, SUB * q + j : SUB * q + j + 1], shape) for g in live}
            for j in range(SUB)
        ]
        d = {(i, j): jnp.broadcast_to(cols[j][q][i : i + 1, :], shape) for j in range(SUB) for i in range(j, SUB)}
        scale, low, inv = [], {}, {}
        for j in range(SUB):
            s = lax.rsqrt(d[j, j])
            scale.append(s)
            for i in range(j + 1, SUB):
                low[i, j] = d[i, j] * s
            for k in range(j + 1, SUB):
                for i in range(k, SUB):
                    d[i, k] = d[i, k] - low[i, j] * low[k, j]
            inv[j, j] = s
            for k in range(j):
                total = low[j, k] * inv[k, k]
                for i in range(k + 1, j):
                    total = total + low[j, i] * inv[i, k]
                inv[j, k] = -(total * s)
        block = (lane >= SUB * q) & (lane < SUB * (q + 1))
        unit = jnp.where(lane == sub + SUB * q, 1.0, 0.0)
        row_lo = jnp.where(block, unit, lo[q])
        new_lo, new_hi = jnp.zeros(shape, jnp.float32), jnp.zeros(shape, jnp.float32)
        for j in range(SUB):
            weight = jnp.zeros(shape, jnp.float32)
            for i in range(j, SUB):
                weight = jnp.where(sub == i, inv[i, j], weight)
            new_lo = new_lo + weight * jnp.broadcast_to(row_lo[j : j + 1, :], shape)
            new_hi = new_hi + weight * jnp.broadcast_to(hi[q][j : j + 1, :], shape)
        lo[q], hi[q] = new_lo, new_hi
        below = range(q + 1, groups)
        for g in below:
            lo[g] = jnp.where(block, 0.0, lo[g])
        for j in range(SUB):
            u_lo = jnp.broadcast_to(lo[q][j : j + 1, :], shape)
            u_hi = jnp.broadcast_to(hi[q][j : j + 1, :], shape)
            for g in below:
                m = cols[j][g] * scale[j]
                for k in range(j + 1, SUB):
                    cols[k][g] = cols[k][g] - m * low[k, j]
                lo[g] = lo[g] - m * u_lo
                hi[g] = hi[g] - m * u_hi
    for g in range(groups):
        lo[g] = jnp.where((lane < STEP) & (lane > sub + SUB * g), 0.0, lo[g])
    return jnp.concatenate(
        [jnp.concatenate([lo[g], hi[g]], axis=1) for g in range(groups)], axis=0
    )


def factor(work, prev):
    row_id = lax.broadcasted_iota(jnp.int32, (NB, NB), 0)
    lane_id = lax.broadcasted_iota(jnp.int32, (NB, NB), 1)
    panel_lane = lax.broadcasted_iota(jnp.int32, (STEP, NB), 1)
    prev[...] = jnp.zeros((STEP, NB), jnp.float32)

    def body(step, carry):
        start = pl.multiple_of(step * STEP, STEP)
        stop = start + STEP
        turn = lax.rem(NB - start, NB)
        last = prev[...]
        rolled = pltpu.roll(last, turn, axis=1)
        panel = pltpu.roll(work[pl.ds(start, STEP), :], turn, axis=1)
        panel = jnp.where((panel_lane >= NB - STEP) & (step > 0), 0.0, panel)
        panel = panel - thin_dot(rolled[:, :STEP], rolled)
        panel = pltpu.roll(factor_panel(panel), start, axis=1)
        below = jnp.where(panel_lane >= stop, last, 0.0)
        spent = (row_id >= stop) & (lane_id >= start - STEP) & (lane_id < start)
        work[...] = jnp.where(spent, 0.0, work[...]) - thin_dot(below, last)
        work[pl.ds(start, STEP), :] = panel
        prev[...] = panel
        return carry

    lax.fori_loop(0, NB // STEP, body, 0)
    return jnp.where(lane_id <= row_id, work[...], 0.0)


def tiles_from(ids, pieces, k, out):
    y = ids[2] // 4
    for j in range(4):
        at = pl.multiple_of(lax.rem(y - j + 4, 4) * 64, 64)
        out[pl.ds(at, 64), :] = tile_from(pieces.at[j, k])


def first_tile(ref):
    return jnp.concatenate([ref[pl.ds(q, NB, stride=4), :] for q in range(2)], axis=1)


def first_kernel(ids, flat, inv_ref, rows_ref, slab_ref, work, prev, sems):
    rows = pltpu.make_async_copy(flat.at[pl.ds(0, 4 * NB), :], rows_ref, sems.at[0])
    start = pl.multiple_of(ids[2] * 8 * NB, 8 * NB)
    slab = pltpu.make_async_copy(flat.at[pl.ds(start, 8 * NB), :], slab_ref, sems.at[1])
    rows.start()
    slab.start()
    rows.wait()

    @pl.when((ids[0] == 0) & (ids[1] == 0))
    def _():
        work[...] = first_tile(rows_ref)
        inv = factor(work, prev)
        for q in range(2):
            inv_ref[pl.ds(q, NB, stride=2), :] = inv[:, q * LANES : (q + 1) * LANES]

    slab.wait()


def second_kernel(ids, own, other, inv0_ref, up_ref, inv_ref, lower, work, prev):
    def place(upper, under):
        tiles_from(ids, upper, 0, inv0_ref)
        tiles_from(ids, under, 0, lower)
        tiles_from(ids, under, 1, work)

    pl.when(ids[0] == 0)(lambda: place(own, other))
    pl.when(ids[0] != 0)(lambda: place(other, own))
    up = dot(inv0_ref[...], lower[...], 1, 1)
    up_ref[...] = up
    work[...] = work[...] - dot(up, up, 0, 0)
    inv_ref[...] = factor(work, prev)


def last_kernel(ids, slab, own_rows, other_rows, x0, x1, inv0_ref, up_ref, inv1_ref, out_ref):
    row, col, depth = ids[0], ids[1], ids[2]
    rows_a, rows_b = wide_from(own_rows), wide_from(other_rows)
    rows0 = jnp.where(row == 0, rows_a, rows_b)
    rows1 = jnp.where(row == 0, rows_b, rows_a)
    row_id = lax.broadcasted_iota(jnp.int32, (2 * NB, NB), 0)
    tile_id = 4 * depth + 2 * (row_id // NB) + row
    inv0, up, inv1 = inv0_ref[...], up_ref[...], inv1_ref[...]
    p0 = dot(tile_from(x0), inv0, 1, 1)
    q0 = dot(inv0, rows0)
    b0 = jnp.where(tile_id > 0, p0, 0.0)
    p1 = jnp.where(tile_id >= 1, dot(tile_from(x1) - dot(b0, up), inv1, 1, 1), 0.0)
    q1 = dot(inv1, rows1 - dot(up, q0, 0, 0))
    b1 = jnp.where(tile_id > 1, p1, 0.0)
    change = dot(b0, q0) + dot(b1, q1)
    for q in range(4):
        piece = slab[pl.ds(q, 2 * NB, stride=4), :] - change[:, q * LANES : (q + 1) * LANES]
        if q < 2:
            lanes = slice(q * LANES, (q + 1) * LANES)
            piece = jnp.where(col == 0, p0[:, lanes], jnp.where(col == 1, p1[:, lanes], piece))
        out_ref[pl.ds(q, 2 * NB, stride=4), :] = piece


def whole(shape):
    return pl.BlockSpec(shape, lambda i, ids: (0,) * len(shape))


def call(kernel, ids, args, specs, outs, scratch, flops, vmem):
    return pl.pallas_call(
        kernel,
        out_shape=[jax.ShapeDtypeStruct(s, jnp.float32) for s in outs],
        grid_spec=pltpu.PrefetchScalarGridSpec(
            num_scalar_prefetch=1,
            grid=(1,),
            in_specs=specs,
            out_specs=[whole(s) for s in outs],
            scratch_shapes=scratch,
        ),
        compiler_params=pltpu.CompilerParams(vmem_limit_bytes=vmem << 20),
        cost_estimate=pl.CostEstimate(flops=flops, bytes_accessed=1 << 20, transcendentals=0),
    )(ids, *args)


def choose(col, table):
    out = table[0][0]
    for value, cols in table[1:]:
        for c in cols:
            out = jnp.where(col == c, value, out)
    return out


def shards(gram_slab):
    row = lax.axis_index("row")
    col = lax.axis_index("col")
    depth = lax.axis_index("depth")
    ids = jnp.stack([row, col, depth]).astype(jnp.int32)
    flat = gram_slab.reshape(32 * NB * 4, LANES)

    def swap(x):
        return lax.ppermute(x, "row", [(0, 1), (1, 0)])

    def send(x, pairs):
        return lax.ppermute(x, "col", pairs)

    def far(x):
        return send(x, [(0, 3), (1, 4)]), send(x, [(0, 5), (1, 6)])

    def near(x):
        ahead = [(0, 1), (3, 4), (5, 6), (1, 2), (4, 5), (6, 7)]
        return send(x, ahead), send(x, [(0, 7), (3, 2), (1, 0), (4, 3)])

    def held_of(x, ahead, back):
        return choose(col, [(x, ()), (ahead, (3, 4)), (back, (5, 6))])

    def both_of(x, ahead, back):
        return (
            choose(col, [(x, ()), (ahead, (1, 4, 6)), (back, (2, 7))]),
            choose(col, [(x, ()), (ahead, (2, 5, 7)), (back, (0, 3))]),
        )

    square = whole((NB, NB))
    scratch = [pltpu.VMEM((NB, NB), jnp.float32), pltpu.VMEM((STEP, NB), jnp.float32)]
    inv0, own_rows, block = call(
        first_kernel,
        ids,
        (flat,),
        [pl.BlockSpec(memory_space=pl.ANY)],
        [(512, LANES), (1024, LANES), (2048, LANES)],
        scratch + [pltpu.SemaphoreType.DMA((2,))],
        10**10,
        40,
    )

    strip = block.reshape(512, 4, LANES)[:, :2].reshape(1024, LANES)
    y = depth // 4
    tile = lax.dynamic_slice_in_dim(own_rows, y * 256, 256, 0).reshape(64, 4, LANES)[:, :2]
    inv0 = lax.dynamic_slice_in_dim(inv0, y * 128, 128, 0)
    tile = jnp.where((row == 0) & (col == 0), inv0, tile.reshape(128, LANES))
    strip, tile = lax.optimization_barrier((strip, tile))
    x_a = send(strip, [(0, 5), (1, 4)])
    tile = held_of(tile, *far(tile))
    mine = jnp.stack(both_of(tile, *near(tile)))
    x_a, mine = lax.optimization_barrier((x_a, mine))
    held = choose(col, [(x_a, ()), (strip, (0, 1))])
    x_b = send(held, [(0, 1), (5, 6), (4, 3)])
    x_c = send(held, [(1, 0), (5, 4), (4, 5)])
    own = jnp.stack(
        [mine] + [lax.ppermute(mine, "depth", [(d, (d + 4 * j) % 16) for d in range(16)]) for j in (1, 2, 3)]
    )
    x_c, x_b, own = lax.optimization_barrier((x_c, x_b, own))
    other = swap(own)

    own, other, own_rows = lax.optimization_barrier((own, other, own_rows))
    other_rows = swap(own_rows)
    held = choose(col, [(x_b, ()), (x_c, (0, 4, 5))])
    x_d = send(held, [(4, 3), (6, 7), (3, 2), (5, 6)])
    x_e = send(held, [(1, 2), (0, 7)])
    inv0, up, inv1 = call(
        second_kernel, ids, (own, other), [whole(own.shape)] * 2, [(NB, NB)] * 3, scratch[:1] + scratch, 10**10, 12
    )
    x_d, x_e, inv1 = lax.optimization_barrier((x_d, x_e, inv1))
    x0 = choose(col, [(x_d, ()), (strip, (0,)), (x_b, (1, 6)), (x_e, (2,)), (x_a, (5,)), (x_c, (4,))])
    x1 = choose(col, [(x_d, ()), (x_c, (0, 5)), (strip, (1,)), (x_b, (3,)), (x_a, (4,)), (x_e, (7,))])
    (out,) = call(
        last_kernel,
        ids,
        (block, own_rows, other_rows, x0, x1, inv0, up, inv1),
        [whole((2048, LANES))] + [whole((1024, LANES))] * 4 + [square] * 3,
        [(2048, LANES)],
        [],
        10**9,
        32,
    )
    return out.reshape(2, 1, NB, 2, 1, NB)


def solution(mesh):
    in_specs = (P(None, "row", None, None, "col", None),)
    out_specs = P("depth", "row", None, None, "col", None)
    return jax.shard_map(shards, mesh=mesh, in_specs=in_specs, out_specs=out_specs, check_vma=False)
```
